32 devices in a mesh: tile: 16 (over z, x, core), trc: 2 (over y).
Axes of the slice: x: 2, y: 2, z: 4, core: 2. Of those that a mesh axis runs over, the one named last changes fastest.
Arguments:
- tracers: float32 [32, 47, 96, 256], P('trc', None, 'tile'), may hold values from -6 to 6
- courant: float32 [47, 96, 256], P(None, 'tile'), may hold values from -0.4 to 0.4
- vertical_mix: float32 [47, 96, 256], P(None, 'tile'), may hold values from 0.02 to 0.12
- kernel_profile: float32 [47], replicated, may hold values from 0.25 to 1.75
- obs_cell: int32 [32768], P('tile'), may hold values from 0 to 1535
- obs_top: int32 [32768], P('tile'), may hold values from 1 to 47
- obs_count: int32 [16], P('tile'), may hold values from 1 to 2048, 16384 in all
- innovation: float32 [32768], P('tile'), may hold values from -6 to 6
- obs_error: float32 [32768], P('tile'), may hold values from 0.3 to 3
- prior_precision: float32 [32], replicated, may hold values from 0.5 to 2
Outputs:
- fields: float32 [32, 47, 96, 256], P('trc', None, 'tile')
- update: float32 [32], replicated
- misfit: float32 [32768], P('tile')
The draws below stay inside these ranges and needn't reach their ends.
Inputs may be any that keep to these rules, and one draw needn't show every extreme that they name: obs_cell counts cells of the observation's own tile. `obs_count`: the counts sum to 16384 and some tile is full.
All inputs are finite; a program needn't handle non-finite values. No bound on the sum of `obs_count` on one device may be relied on, other than what follows from the above.
Results may differ from the reference program's by a relative error of at most 0.0003.
Values sent between devices are 32-bit elements; how exact they have to be, the bound alone decides.
A program may use at most 192 MiB of HBM per device.

```python
import math
import jax
import jax.numpy as jnp
import numpy as np
from jax import lax

TRACERS = 32
LEV = 47
LAT = 256
CLON = 6
OBS_CAP = 2048
STEPS = 3
NLON = 96
OBS = 32768
N_TILE = 16


def set_ends(array, stream_key, low, high):
    longest = array.shape.index(max(array.shape))
    spots = []
    for shift in (0, 1):
        where = [jax.random.randint(jax.random.fold_in(stream_key, axis), (), 0, length) for axis, length in enumerate(array.shape)]
        where[longest] = (where[longest] + shift) % array.shape[longest]
        spots.append(tuple(where))
    return array.at[spots[0]].set(low).at[spots[1]].set(high)


def block_scale(key, extent, cuts, low, largest):
    def one(axis_at, shards_of):
        heights = jax.random.uniform(jax.random.fold_in(jax.random.fold_in(key, 6), axis_at), (shards_of,), jnp.float32, low / len(cuts), largest / len(cuts))
        return jnp.repeat(jnp.exp(heights), extent[axis_at] // shards_of).reshape((-1,) + (1,) * (len(extent) - axis_at - 1))

    level = one(*cuts[0])
    for cut in cuts[1:]:
        level = level * one(*cut)
    return level


def profile(number_of, total, most, skew):
    weights = [(1 << 20) // math.isqrt(grade ** skew) + 1 for grade in range(2, number_of + 1)]
    surplus, holding = total - most - (number_of - 1), [1] * (number_of - 1)
    while surplus > 0:
        candidates = [i for i in range(number_of - 1) if holding[i] < most]
        pool, left = sum([weights[i] for i in candidates]), surplus
        for i in candidates:
            addition = min(most - holding[i], max(1, left * weights[i] // pool), surplus)
            holding[i] = holding[i] + addition
            surplus = surplus - addition
    return np.array([most] + holding)


def uneven_parts(stream_key, number_of, total, limit, slope):
    if number_of == 2:
        one = jax.random.randint(stream_key, (), max(1, total - limit), min(limit, total - 1) + 1)
        return jnp.stack([one, total - one])
    tallies = jnp.asarray(profile(number_of, total, limit, slope), jnp.int32)
    couples = (number_of - 1) // 2
    donor, taker = tallies[1:1 + 2 * couples:2], tallies[2:2 + 2 * couples:2]
    margin = jnp.minimum(donor - 1, limit - taker)
    passed = jax.random.randint(jax.random.fold_in(stream_key, 1), (couples,), 0, 1 << 20) % (margin + 1)
    tallies = tallies.at[1:1 + 2 * couples:2].set(donor - passed).at[2:2 + 2 * couples:2].set(taker + passed)
    return tallies[jax.random.permutation(jax.random.fold_in(stream_key, 2), number_of)]


def bell_draw(rng, dims, scale, most, pieces=(), kind=jnp.bfloat16):
    drawn = scale * jax.random.normal(rng, dims, jnp.float32)
    if pieces:
        drawn = drawn * block_scale(rng, dims, pieces, -0.22, 0.18)
    return jnp.clip(drawn, -most, most).astype(kind)


def setup_inputs(seed: int = 0) -> dict:
    splits = jax.random.split(jax.random.key(seed), 11)
    tracers = bell_draw(splits[0], (TRACERS, LEV, NLON, LAT), 1.0, 6.0, ((0, 2), (2, 16)), jnp.float32)
    courant = jnp.clip(jax.random.uniform(splits[1], (LEV, NLON, LAT), jnp.float32, -0.4, 0.4) * block_scale(splits[1], (LEV, NLON, LAT), ((1, 16),), -0.4, 0.0), -0.4, 0.4)
    vertical_mix = jnp.clip(0.02 + 0.09999999776482582 * jax.random.uniform(splits[2], (LEV, NLON, LAT), jnp.float32) ** block_scale(splits[2], (LEV, NLON, LAT), ((1, 16),), -0.2, 0.2), 0.02, 0.12)
    kernel_profile = jnp.clip(1.0 + 0.15 * jax.random.normal(splits[3], (LEV,), jnp.float32), 0.25, 1.75)
    obs_cell = set_ends(jax.random.randint(splits[4], (OBS,), 0, CLON * LAT), jax.random.fold_in(splits[4], 1), 0, (CLON * LAT) - 1).astype(jnp.int32)
    obs_top = set_ends(jax.random.randint(splits[5], (OBS,), 1, LEV + 1), jax.random.fold_in(splits[5], 1), 1, LEV).astype(jnp.int32)
    obs_count = uneven_parts(splits[6], N_TILE, N_TILE * OBS_CAP // 2, OBS_CAP, 2).astype(jnp.int32)
    innovation = bell_draw(splits[7], (OBS,), 1.0, 6.0, ((0, 16),), jnp.float32)
    obs_error = jnp.clip(jnp.exp(math.log(3.0) - 2.3025851 * jax.random.uniform(splits[8], (OBS,), jnp.float32) ** block_scale(splits[8], (OBS,), ((0, 16),), -0.2, 0.2)), 0.3, 3.0)
    prior_precision = jnp.clip(jnp.exp(jax.random.uniform(splits[9], (TRACERS,), jnp.float32, math.log(0.5), math.log(2.0))), 0.5, 2.0)
    return {"tracers": tracers, "courant": courant, "vertical_mix": vertical_mix, "kernel_profile": kernel_profile, "obs_cell": obs_cell, "obs_top": obs_top, "obs_count": obs_count, "innovation": innovation, "obs_error": obs_error, "prior_precision": prior_precision}


HORIZ = 0.05

def advance(padded, wind_pad, mix_pad):
    centre = padded[:, :, 1:-1]
    left = padded[:, :, :-2]
    right = padded[:, :, 2:]
    wind_here = wind_pad[:, 1:-1]
    wind_east = wind_pad[:, 2:]
    mixing = mix_pad[:, 1:-1]
    inflow = jnp.maximum(wind_here, 0.0) * left + jnp.minimum(wind_here, 0.0) * centre
    outflow = jnp.maximum(wind_east, 0.0) * centre + jnp.minimum(wind_east, 0.0) * right
    north = jnp.concatenate([centre[..., 1:], centre[..., -1:]], -1)
    south = jnp.concatenate([centre[..., :1], centre[..., :-1]], -1)
    above = jnp.concatenate([centre[:, 1:], centre[:, -1:]], 1)
    below = jnp.concatenate([centre[:, :1], centre[:, :-1]], 1)
    return centre + inflow - outflow + HORIZ * (left + right - 2.0 * centre) + HORIZ * (north + south - 2.0 * centre) + mixing * (above + below - 2.0 * centre)

def periodic(field, axis):
    width = field.shape[axis]
    return jnp.concatenate([lax.slice_in_dim(field, width - 1, width, axis=axis), field, lax.slice_in_dim(field, 0, 1, axis=axis)], axis)

def reference(tracers, courant, vertical_mix, kernel_profile, obs_cell, obs_top, obs_count, innovation, obs_error, prior_precision):
    fields = tracers
    wind_pad = periodic(courant, 1)
    mix_pad = periodic(vertical_mix, 1)
    for step in range(STEPS):
        fields = advance(periodic(fields, 2), wind_pad, mix_pad)
    cells = obs_cell.reshape(N_TILE, OBS_CAP)
    tops = obs_top.reshape(N_TILE, OBS_CAP)
    levels = jnp.arange(LEV, dtype=jnp.int32)

    def per_tile(index):
        block = lax.dynamic_slice_in_dim(fields, index * CLON, CLON, 2).reshape(TRACERS, LEV, CLON * LAT)
        values = block[:, :, cells[index]]
        weights = kernel_profile[:, None] * (levels[:, None] < tops[index][None, :]).astype(jnp.float32)
        return jnp.einsum('tlk,lk->tk', values, weights, precision=lax.Precision.HIGHEST)
    jacobian = lax.map(per_tile, jnp.arange(N_TILE, dtype=jnp.int32))
    slots = jnp.arange(OBS_CAP, dtype=jnp.int32)
    live = (slots[None, :] < obs_count[:, None]).astype(jnp.float32)
    innov = innovation.reshape(N_TILE, OBS_CAP)
    weight = live / obs_error.reshape(N_TILE, OBS_CAP)
    weighted = jacobian * weight[:, None, :]
    gram = jnp.einsum('ntk,nsk->ts', weighted, jacobian, precision=lax.Precision.HIGHEST) + jnp.diag(prior_precision)
    gradient = jnp.einsum('ntk,nk->t', weighted, innov, precision=lax.Precision.HIGHEST)
    update = jnp.linalg.solve(gram, gradient)
    fitted = jnp.einsum('t,ntk->nk', update, jacobian, precision=lax.Precision.HIGHEST)
    misfit = (live * (innov - fitted)).reshape(OBS_CAP * N_TILE)
    return (fields, update, misfit)
```

```python
import functools
import math

import jax
import jax.numpy as jnp
from jax import lax
from jax.experimental import pallas as pl
from jax.experimental.pallas import tpu as pltpu
from jax.sharding import PartitionSpec as P

HORIZ = 0.05
STEPS = 3
GROUP = 8
LANES = 128
CHUNK = 256
MESH = pl.DeviceIdType.MESH


def split_group(size):
    return max(d for d in range(1, math.isqrt(size) + 1) if size % d == 0)


def pieces_of(x, count):
    out = []
    for _ in range(count - 1):
        scaled = x * 65537.0
        piece = scaled - (scaled - x)
        out.append(piece.astype(jnp.bfloat16))
        x = x - piece
    return out + [x.astype(jnp.bfloat16)]


def kernel(
    n_tile, n_trc,
    tr_hbm, u_hbm, m_hbm, kp, cell, top, count, innov, err, prior,
    out_hbm, upd, misfit,
    a0, a1, a2, a3, u, m, c_mid, c_west, c_east, c_vert, onehot, staged, jac, g1, g2,
    own_sem, out_sem, w_send, w_recv, e_send, e_recv,
    wind_send, wind_recv, j_send, j_recv, g1_send, g1_recv, g2_send, g2_recv,
):
    levels, cols, group, lat = out_hbm.shape
    chunks = jac.shape[1]
    per = CHUNK // LANES
    tile = lax.axis_index("tile")
    trc = lax.axis_index("trc")
    ga = split_group(n_tile)
    gb = n_tile // ga
    rank_b = tile // ga
    rank_a = tile % ga
    east = (tile + 1) % n_tile
    west = (tile + n_tile - 1) % n_tile
    a_peers = [rank_b * ga + (rank_a + d) % ga for d in range(1, ga)]
    b_peers = [((rank_b + d) % gb) * ga + rank_a for d in range(1, gb)]
    t_peers = [(trc + d) % n_trc for d in range(1, n_trc)]

    barrier = pltpu.get_barrier_semaphore()
    for peer in [east, west] + a_peers + b_peers:
        pl.semaphore_signal(barrier, inc=1, device_id={"tile": peer}, device_id_type=MESH)
    for peer in t_peers:
        pl.semaphore_signal(barrier, inc=1, device_id={"trc": peer}, device_id_type=MESH)

    own = [
        pltpu.make_async_copy(tr_hbm, a0.at[:, pl.ds(STEPS, cols)], own_sem.at[0]),
        pltpu.make_async_copy(u_hbm, u.at[pl.ds(STEPS, cols)], own_sem.at[1]),
        pltpu.make_async_copy(m_hbm, m.at[pl.ds(STEPS, cols)], own_sem.at[2]),
    ]
    for copy in own:
        copy.start()
    pl.semaphore_wait(barrier, 2 + len(a_peers) + len(b_peers) + len(t_peers))

    def remote(src, dst, send, recv, **where):
        return pltpu.make_async_remote_copy(
            src_ref=src, dst_ref=dst, send_sem=send, recv_sem=recv,
            device_id=where, device_id_type=MESH,
        )

    far = STEPS + cols
    winds = [
        remote(u_hbm.at[pl.ds(0, STEPS)], u.at[pl.ds(far, STEPS)], wind_send.at[0], wind_recv.at[0], tile=west),
        remote(m_hbm.at[pl.ds(0, STEPS - 1)], m.at[pl.ds(far, STEPS - 1)], wind_send.at[1], wind_recv.at[1], tile=west),
        remote(u_hbm.at[pl.ds(cols - 2, 2)], u.at[pl.ds(1, 2)], wind_send.at[2], wind_recv.at[2], tile=east),
        remote(m_hbm.at[pl.ds(cols - 2, 2)], m.at[pl.ds(1, 2)], wind_send.at[3], wind_recv.at[3], tile=east),
    ]
    for copy in winds:
        copy.start()

    def to_west(l):
        return remote(tr_hbm.at[l, pl.ds(0, STEPS)], a0.at[l, pl.ds(far, STEPS)], w_send.at[l], w_recv.at[l], tile=west)

    def to_east(l):
        return remote(tr_hbm.at[l, pl.ds(cols - STEPS, STEPS)], a0.at[l, pl.ds(0, STEPS)], e_send.at[l], e_recv.at[l], tile=east)

    def launch(l, carry):
        to_west(l).start()
        to_east(l).start()
        return carry

    lax.fori_loop(0, levels, launch, 0)

    rows = lax.broadcasted_iota(jnp.int32, (lat, LANES), 0)

    def build(n, carry):
        for h in range(per):
            here = jnp.broadcast_to(cell[pl.ds(n * per + h, 1), :], (lat, LANES))
            for x in range(cols):
                hit = here == rows + x * lat
                onehot[n, x, :, h * LANES:(h + 1) * LANES] = hit.astype(jnp.float32).astype(jnp.bfloat16)
        return carry

    lax.fori_loop(0, chunks, build, 0)
    staged[...] = jnp.zeros_like(staged)
    jac[trc] = jnp.zeros(jac.shape[1:], jnp.float32)

    for copy in own:
        copy.wait()
    for copy in winds:
        copy.wait()
    for x in range(cols + 4):
        here, there, mix = u[x + 1], u[x + 2], m[x + 1]
        c_west[x] = jnp.maximum(here, 0.0) + HORIZ
        c_east[x] = HORIZ - jnp.minimum(there, 0.0)
        c_mid[x] = (1.0 - 4.0 * HORIZ) + jnp.minimum(here, 0.0) - jnp.maximum(there, 0.0) - 2.0 * mix
        c_vert[x] = mix

    lane = lax.broadcasted_iota(jnp.int32, (group, lat), 1)
    first = lane == 0
    last = lane == lat - 1

    def advance(src, l, shift, width, store):
        lo = lax.max(l - 1, 0)
        hi = lax.min(l + 1, levels - 1)

        def coef(ref, x):
            return jnp.broadcast_to(ref[x + shift, pl.ds(l, 1), :], (group, lat))

        for x in range(width):
            c = src[l, x + 1]
            south = jnp.where(first, c, pltpu.roll(c, 1, 1))
            north = jnp.where(last, c, pltpu.roll(c, lat - 1, 1))
            store(
                x,
                coef(c_mid, x) * c
                + coef(c_west, x) * src[l, x]
                + coef(c_east, x) * src[l, x + 2]
                + HORIZ * (south + north)
                + coef(c_vert, x) * (src[lo, x + 1] + src[hi, x + 1]),
            )

    def out_copy(l):
        return pltpu.make_async_copy(a3.at[l], out_hbm.at[l], out_sem.at[l])

    def gather(base):
        def one(n, carry):
            total = jnp.zeros((2 * GROUP * group, CHUNK), jnp.float32)
            for x in range(cols):
                total += jnp.dot(
                    staged[x].reshape(2 * GROUP * group, lat), onehot[n, x],
                    preferred_element_type=jnp.float32,
                )
            parts = total.reshape(2, GROUP, group, CHUNK)
            tops = jnp.concatenate([top[pl.ds(n * per + h, 1), :] for h in range(per)], axis=1)
            acc = jac[trc, n]
            for i in range(GROUP):
                level = base + i
                scale = jnp.where(level < tops, kp[lax.min(level, levels - 1)], 0.0)
                acc += scale * (parts[0, i] + parts[1, i])
            jac[trc, n] = acc
            return carry

        lax.fori_loop(0, chunks, one, 0)

    def sweep(i, carry):
        @pl.when(i < levels)
        def _():
            to_west(i).wait_recv()
            to_east(i).wait_recv()

        @pl.when((i >= 1) & (i <= levels))
        def _():
            l = i - 1

            def store(x, v):
                a1[l, x] = v

            advance(a0, l, 0, cols + 4, store)

        @pl.when((i >= 2) & (i <= levels + 1))
        def _():
            l = i - 2

            def store(x, v):
                a2[l, x] = v

            advance(a1, l, 1, cols + 2, store)

        @pl.when(i >= 3)
        def _():
            l = i - 3
            slot = l % GROUP

            def store(x, v):
                a3[l, x] = v
                big, small = pieces_of(v, 2)
                staged[x, 0, slot] = big
                staged[x, 1, slot] = small

            advance(a2, l, 2, cols, store)
            out_copy(l).start()

            @pl.when((slot == GROUP - 1) | (l == levels - 1))
            def _():
                gather(l - slot)

        return carry

    lax.fori_loop(0, levels + STEPS, sweep, 0)

    swaps = [
        remote(jac.at[trc], jac.at[trc], j_send.at[d], j_recv.at[d], trc=peer)
        for d, peer in enumerate(t_peers)
    ]
    for copy in swaps:
        copy.start()

    slot_of = lax.broadcasted_iota(jnp.int32, misfit.shape, 0) * LANES + lax.broadcasted_iota(jnp.int32, misfit.shape, 1)
    live = jnp.where(slot_of < count[0], 1.0, 0.0)
    weight = live / err[...]
    inn = innov[...]
    state = n_trc * group

    for copy in swaps:
        copy.wait()

    def wide(value, n):
        return jnp.concatenate([value[n * per + h:n * per + h + 1, :] for h in range(per)], axis=1)

    pad = 16
    gram = jnp.zeros((state, state + pad), jnp.float32)
    pad_row = lax.broadcasted_iota(jnp.int32, (pad, CHUNK), 0)
    for n in range(chunks):
        jn = jac[:, n].reshape(state, CHUNK)
        left = jnp.concatenate(pieces_of(jn * wide(weight, n), 3), axis=0)
        extra = jnp.where(pad_row == 0, jnp.broadcast_to(wide(inn, n), (pad, CHUNK)), 0.0)
        for right in pieces_of(jnp.concatenate([jn, extra], axis=0), 3):
            prod = lax.dot_general(left, right, (((1,), (1,)), ((), ())), preferred_element_type=jnp.float32)
            gram += prod[:state] + prod[state:2 * state] + prod[2 * state:]

    def reduce(buf, part, rank, peers, send, recv):
        buf[rank] = jnp.concatenate([part, jnp.zeros((state, LANES - part.shape[1]), jnp.float32)], axis=1) if part.shape[1] < LANES else part
        copies = [
            remote(buf.at[rank], buf.at[rank], send.at[d], recv.at[d], tile=peer)
            for d, peer in enumerate(peers)
        ]
        for copy in copies:
            copy.start()
        for copy in copies:
            copy.wait()
        total = buf[0]
        for k in range(1, buf.shape[0]):
            total += buf[k]
        return total

    total = reduce(g1, gram, rank_a, a_peers, g1_send, g1_recv)
    total = reduce(g2, total, rank_b, b_peers, g2_send, g2_recv)

    sub = lax.broadcasted_iota(jnp.int32, (state, LANES), 0)
    lan = lax.broadcasted_iota(jnp.int32, (state, LANES), 1)
    diag = jnp.concatenate([prior[...], jnp.zeros((1, LANES - state), jnp.float32)], axis=1)
    mat = total + jnp.where(sub == lan, jnp.broadcast_to(diag, (state, LANES)), 0.0)
    for j in range(state):
        row = mat[j:j + 1, :]
        scaled = row / jnp.broadcast_to(row[:, j:j + 1], (1, LANES))
        column = jnp.broadcast_to(mat[:, j:j + 1], (state, LANES))
        mat = jnp.where(sub == j, jnp.broadcast_to(scaled, (state, LANES)), mat - column * scaled)
    answer = mat[:, state:state + 1]
    flat = jnp.sum(jnp.where(sub == lan, jnp.broadcast_to(answer, (state, LANES)), 0.0), axis=0, keepdims=True)
    upd[...] = flat[:, :state]

    for n in range(chunks):
        fit = jnp.sum(jac[:, n].reshape(state, CHUNK) * answer, axis=0, keepdims=True)
        for h in range(per):
            r = n * per + h
            misfit[r:r + 1, :] = live[r:r + 1, :] * (inn[r:r + 1, :] - fit[:, h * LANES:(h + 1) * LANES])


    def drain(l, carry):
        to_west(l).wait_send()
        to_east(l).wait_send()
        out_copy(l).wait()
        return carry

    lax.fori_loop(0, levels, drain, 0)


def per_device(
    n_tile, n_trc,
    tracers, courant, vertical_mix, kernel_profile, obs_cell, obs_top,
    obs_count, innovation, obs_error, prior_precision,
):
    group, levels, cols, lat = tracers.shape
    cap = obs_cell.shape[0]
    rows = cap // LANES
    chunks = cap // CHUNK
    state = group * n_trc
    ga = split_group(n_tile)
    gb = n_tile // ga
    f32 = jnp.float32
    dma = pltpu.SemaphoreType.DMA
    any_spec = pl.BlockSpec(memory_space=pl.ANY)
    vmem = pl.BlockSpec(memory_space=pltpu.VMEM)
    smem = pl.BlockSpec(memory_space=pltpu.SMEM)
    coef = pltpu.VMEM((cols + 4, levels, lat), f32)
    wind = pltpu.VMEM((cols + 2 * STEPS, levels, lat), f32)
    fields, update, misfit = pl.pallas_call(
        functools.partial(kernel, n_tile, n_trc),
        out_shape=(
            jax.ShapeDtypeStruct((levels, cols, group, lat), f32),
            jax.ShapeDtypeStruct((1, state), f32),
            jax.ShapeDtypeStruct((rows, LANES), f32),
        ),
        in_specs=[any_spec] * 3 + [smem, vmem, vmem, smem, vmem, vmem, vmem],
        out_specs=(any_spec, vmem, vmem),
        scratch_shapes=[
            pltpu.VMEM((levels, cols + 6, group, lat), f32),
            pltpu.VMEM((levels, cols + 4, group, lat), f32),
            pltpu.VMEM((levels, cols + 2, group, lat), f32),
            pltpu.VMEM((levels, cols, group, lat), f32),
            wind, wind, coef, coef, coef, coef,
            pltpu.VMEM((chunks, cols, lat, CHUNK), jnp.bfloat16),
            pltpu.VMEM((cols, 2, GROUP, group, lat), jnp.bfloat16),
            pltpu.VMEM((n_trc, chunks, group, CHUNK), f32),
            pltpu.VMEM((ga, state, LANES), f32),
            pltpu.VMEM((gb, state, LANES), f32),
            dma((3,)), dma((levels,)),
            dma((levels,)), dma((levels,)), dma((levels,)), dma((levels,)),
            dma((4,)), dma((4,)),
            dma((max(1, n_trc - 1),)), dma((max(1, n_trc - 1),)),
            dma((max(1, ga - 1),)), dma((max(1, ga - 1),)),
            dma((max(1, gb - 1),)), dma((max(1, gb - 1),)),
        ],
        compiler_params=pltpu.CompilerParams(
            collective_id=0, has_side_effects=True, vmem_limit_bytes=56 * 1024 * 1024
        ),
    )(
        jnp.transpose(tracers, (1, 2, 0, 3)),
        jnp.transpose(courant, (1, 0, 2)),
        jnp.transpose(vertical_mix, (1, 0, 2)),
        kernel_profile,
        obs_cell.reshape(rows, LANES),
        obs_top.reshape(rows, LANES),
        obs_count,
        innovation.reshape(rows, LANES),
        obs_error.reshape(rows, LANES),
        prior_precision.reshape(1, state),
    )
    return (jnp.transpose(fields, (2, 0, 1, 3)), update.reshape(state), misfit.reshape(cap))


def solution(mesh):
    in_specs = (
        P("trc", None, "tile", None),
        P(None, "tile", None),
        P(None, "tile", None),
        P(),
        P("tile"),
        P("tile"),
        P("tile"),
        P("tile"),
        P("tile"),
        P(),
    )
    out_specs = (P("trc", None, "tile", None), P(), P("tile"))
    return jax.shard_map(
        functools.partial(per_device, mesh.shape["tile"], mesh.shape["trc"]),
        mesh=mesh, in_specs=in_specs, out_specs=out_specs, check_vma=False,
    )
```

```python
import functools
import math

import jax
import jax.numpy as jnp
from jax import lax
from jax.experimental import pallas as pl
from jax.experimental.pallas import tpu as pltpu
from jax.sharding import PartitionSpec as P

HORIZ = 0.05
STEPS = 3
GROUP = 8
LANES = 128
CHUNK = 256
MESH = pl.DeviceIdType.MESH


def split_group(size):
    return max(d for d in range(1, math.isqrt(size) + 1) if size % d == 0)


def pieces_of(x, count):
    out = []
    for _ in range(count - 1):
        scaled = x * 65537.0
        piece = scaled - (scaled - x)
        out.append(piece.astype(jnp.bfloat16))
        x = x - piece
    return out + [x.astype(jnp.bfloat16)]


def kernel(
    n_tile, n_trc,
    tr_hbm, u_hbm, m_hbm, kp, cell, top, count, innov, err, prior,
    out_hbm, upd, misfit,
    a0, a1, a2, a3, u, m, c_mid, c_west, c_east, c_vert, onehot, staged, jac, g1, g2,
    own_sem, out_sem, w_send, w_recv, e_send, e_recv,
    wind_send, wind_recv, j_send, j_recv, g1_send, g1_recv, g2_send, g2_recv,
):
    levels, cols, group, lat = out_hbm.shape
    chunks = jac.shape[1]
    per = CHUNK // LANES
    tile = lax.axis_index("tile")
    trc = lax.axis_index("trc")
    ga = split_group(n_tile)
    gb = n_tile // ga
    rank_b = tile // ga
    rank_a = tile % ga
    east = (tile + 1) % n_tile
    west = (tile + n_tile - 1) % n_tile
    a_peers = [rank_b * ga + (rank_a + d) % ga for d in range(1, ga)]
    b_peers = [((rank_b + d) % gb) * ga + rank_a for d in range(1, gb)]
    t_peers = [(trc + d) % n_trc for d in range(1, n_trc)]

    barrier = pltpu.get_barrier_semaphore()
    for peer in [east, west] + a_peers + b_peers:
        pl.semaphore_signal(barrier, inc=1, device_id={"tile": peer}, device_id_type=MESH)
    for peer in t_peers:
        pl.semaphore_signal(barrier, inc=1, device_id={"trc": peer}, device_id_type=MESH)

    own = [
        pltpu.make_async_copy(tr_hbm, a0.at[:, pl.ds(STEPS, cols)], own_sem.at[0]),
        pltpu.make_async_copy(u_hbm, u.at[pl.ds(STEPS, cols)], own_sem.at[1]),
        pltpu.make_async_copy(m_hbm, m.at[pl.ds(STEPS, cols)], own_sem.at[2]),
    ]
    for copy in own:
        copy.start()
    pl.semaphore_wait(barrier, 2 + len(a_peers) + len(b_peers) + len(t_peers))

    def remote(src, dst, send, recv, **where):
        return pltpu.make_async_remote_copy(
            src_ref=src, dst_ref=dst, send_sem=send, recv_sem=recv,
            device_id=where, device_id_type=MESH,
        )

    far = STEPS + cols
    winds = [
        remote(u_hbm.at[pl.ds(0, STEPS)], u.at[pl.ds(far, STEPS)], wind_send.at[0], wind_recv.at[0], tile=west),
        remote(m_hbm.at[pl.ds(0, STEPS - 1)], m.at[pl.ds(far, STEPS - 1)], wind_send.at[1], wind_recv.at[1], tile=west),
        remote(u_hbm.at[pl.ds(cols - 2, 2)], u.at[pl.ds(1, 2)], wind_send.at[2], wind_recv.at[2], tile=east),
        remote(m_hbm.at[pl.ds(cols - 2, 2)], m.at[pl.ds(1, 2)], wind_send.at[3], wind_recv.at[3], tile=east),
    ]
    for copy in winds:
        copy.start()

    def to_west(l):
        return remote(tr_hbm.at[l, pl.ds(0, STEPS)], a0.at[l, pl.ds(far, STEPS)], w_send.at[l], w_recv.at[l], tile=west)

    def to_east(l):
        return remote(tr_hbm.at[l, pl.ds(cols - STEPS, STEPS)], a0.at[l, pl.ds(0, STEPS)], e_send.at[l], e_recv.at[l], tile=east)

    def launch(l, carry):
        to_west(l).start()
        to_east(l).start()
        return carry

    lax.fori_loop(0, levels, launch, 0)

    rows = lax.broadcasted_iota(jnp.int32, (lat, LANES), 0)

    def build(n, carry):
        for h in range(per):
            here = jnp.broadcast_to(cell[pl.ds(n * per + h, 1), :], (lat, LANES))
            for x in range(cols):
                hit = here == rows + x * lat
                onehot[n, x, :, h * LANES:(h + 1) * LANES] = hit.astype(jnp.float32).astype(jnp.bfloat16)
        return carry

    lax.fori_loop(0, chunks, build, 0)
    staged[...] = jnp.zeros_like(staged)
    jac[trc] = jnp.zeros(jac.shape[1:], jnp.float32)

    for copy in own:
        copy.wait()
    for copy in winds:
        copy.wait()
    for x in range(cols + 4):
        here, there, mix = u[x + 1], u[x + 2], m[x + 1]
        c_west[x] = jnp.maximum(here, 0.0) + HORIZ
        c_east[x] = HORIZ - jnp.minimum(there, 0.0)
        c_mid[x] = (1.0 - 4.0 * HORIZ) + jnp.minimum(here, 0.0) - jnp.maximum(there, 0.0) - 2.0 * mix
        c_vert[x] = mix

    lane = lax.broadcasted_iota(jnp.int32, (group, lat), 1)
    first = lane == 0
    last = lane == lat - 1

    def advance(src, l, shift, width, store):
        lo = lax.max(l - 1, 0)
        hi = lax.min(l + 1, levels - 1)

        def coef(ref, x):
            return jnp.broadcast_to(ref[x + shift, pl.ds(l, 1), :], (group, lat))

        for x in range(width):
            c = src[l, x + 1]
            south = jnp.where(first, c, pltpu.roll(c, 1, 1))
            north = jnp.where(last, c, pltpu.roll(c, lat - 1, 1))
            store(
                x,
                coef(c_mid, x) * c
                + coef(c_west, x) * src[l, x]
                + coef(c_east, x) * src[l, x + 2]
                + HORIZ * (south + north)
                + coef(c_vert, x) * (src[lo, x + 1] + src[hi, x + 1]),
            )

    def out_copy(l):
        return pltpu.make_async_copy(a3.at[l], out_hbm.at[l], out_sem.at[l])

    def gather(base):
        def one(n, carry):
            total = jnp.dot(
                staged[...].reshape(2 * GROUP * group, cols * lat),
                onehot[n].reshape(cols * lat, CHUNK),
                preferred_element_type=jnp.float32,
            )
            parts = total.reshape(2, GROUP, group, CHUNK)
            tops = jnp.concatenate([top[pl.ds(n * per + h, 1), :] for h in range(per)], axis=1)
            acc = jac[trc, n]
            for i in range(GROUP):
                level = base + i
                scale = jnp.where(level < tops, kp[lax.min(level, levels - 1)], 0.0)
                acc += scale * (parts[0, i] + parts[1, i])
            jac[trc, n] = acc
            return carry

        lax.fori_loop(0, chunks, one, 0)

    def sweep(i, carry):
        @pl.when(i < levels)
        def _():
            to_west(i).wait_recv()
            to_east(i).wait_recv()

        @pl.when((i >= 1) & (i <= levels))
        def _():
            l = i - 1

            def store(x, v):
                a1[l, x] = v

            advance(a0, l, 0, cols + 4, store)

        @pl.when((i >= 2) & (i <= levels + 1))
        def _():
            l = i - 2

            def store(x, v):
                a2[l, x] = v

            advance(a1, l, 1, cols + 2, store)

        @pl.when(i >= 3)
        def _():
            l = i - 3
            slot = l % GROUP

            def store(x, v):
                a3[l, x] = v
                big, small = pieces_of(v, 2)
                staged[0, slot, :, x * lat:(x + 1) * lat] = big
                staged[1, slot, :, x * lat:(x + 1) * lat] = small

            advance(a2, l, 2, cols, store)
            out_copy(l).start()

            @pl.when((slot == GROUP - 1) | (l == levels - 1))
            def _():
                gather(l - slot)

        return carry

    lax.fori_loop(0, levels + STEPS, sweep, 0)

    swaps = [
        remote(jac.at[trc], jac.at[trc], j_send.at[d], j_recv.at[d], trc=peer)
        for d, peer in enumerate(t_peers)
    ]
    for copy in swaps:
        copy.start()

    slot_of = lax.broadcasted_iota(jnp.int32, misfit.shape, 0) * LANES + lax.broadcasted_iota(jnp.int32, misfit.shape, 1)
    live = jnp.where(slot_of < count[0], 1.0, 0.0)
    weight = live / err[...]
    inn = innov[...]
    state = n_trc * group

    for copy in swaps:
        copy.wait()

    def wide(value, n):
        return jnp.concatenate([value[n * per + h:n * per + h + 1, :] for h in range(per)], axis=1)

    pad = 16
    gram = jnp.zeros((state, state + pad), jnp.float32)
    pad_row = lax.broadcasted_iota(jnp.int32, (pad, CHUNK), 0)
    for n in range(chunks):
        jn = jac[:, n].reshape(state, CHUNK)
        left = jnp.concatenate(pieces_of(jn * wide(weight, n), 3), axis=0)
        extra = jnp.where(pad_row == 0, jnp.broadcast_to(wide(inn, n), (pad, CHUNK)), 0.0)
        for right in pieces_of(jnp.concatenate([jn, extra], axis=0), 3):
            prod = lax.dot_general(left, right, (((1,), (1,)), ((), ())), preferred_element_type=jnp.float32)
            gram += prod[:state] + prod[state:2 * state] + prod[2 * state:]

    def reduce(buf, part, rank, peers, send, recv):
        buf[rank] = jnp.concatenate([part, jnp.zeros((state, LANES - part.shape[1]), jnp.float32)], axis=1) if part.shape[1] < LANES else part
        copies = [
            remote(buf.at[rank], buf.at[rank], send.at[d], recv.at[d], tile=peer)
            for d, peer in enumerate(peers)
        ]
        for copy in copies:
            copy.start()
        for copy in copies:
            copy.wait()
        total = buf[0]
        for k in range(1, buf.shape[0]):
            total += buf[k]
        return total

    total = reduce(g1, gram, rank_a, a_peers, g1_send, g1_recv)
    total = reduce(g2, total, rank_b, b_peers, g2_send, g2_recv)

    sub = lax.broadcasted_iota(jnp.int32, (state, LANES), 0)
    lan = lax.broadcasted_iota(jnp.int32, (state, LANES), 1)
    diag = jnp.concatenate([prior[...], jnp.zeros((1, LANES - state), jnp.float32)], axis=1)
    mat = total + jnp.where(sub == lan, jnp.broadcast_to(diag, (state, LANES)), 0.0)
    for j in range(state):
        row = mat[j:j + 1, :]
        scaled = row / jnp.broadcast_to(row[:, j:j + 1], (1, LANES))
        column = jnp.broadcast_to(mat[:, j:j + 1], (state, LANES))
        mat = jnp.where(sub == j, jnp.broadcast_to(scaled, (state, LANES)), mat - column * scaled)
    answer = mat[:, state:state + 1]
    flat = jnp.sum(jnp.where(sub == lan, jnp.broadcast_to(answer, (state, LANES)), 0.0), axis=0, keepdims=True)
    upd[...] = flat[:, :state]

    for n in range(chunks):
        fit = jnp.sum(jac[:, n].reshape(state, CHUNK) * answer, axis=0, keepdims=True)
        for h in range(per):
            r = n * per + h
            misfit[r:r + 1, :] = live[r:r + 1, :] * (inn[r:r + 1, :] - fit[:, h * LANES:(h + 1) * LANES])


    def drain(l, carry):
        to_west(l).wait_send()
        to_east(l).wait_send()
        out_copy(l).wait()
        return carry

    lax.fori_loop(0, levels, drain, 0)


def per_device(
    n_tile, n_trc,
    tracers, courant, vertical_mix, kernel_profile, obs_cell, obs_top,
    obs_count, innovation, obs_error, prior_precision,
):
    group, levels, cols, lat = tracers.shape
    cap = obs_cell.shape[0]
    rows = cap // LANES
    chunks = cap // CHUNK
    state = group * n_trc
    ga = split_group(n_tile)
    gb = n_tile // ga
    f32 = jnp.float32
    dma = pltpu.SemaphoreType.DMA
    any_spec = pl.BlockSpec(memory_space=pl.ANY)
    vmem = pl.BlockSpec(memory_space=pltpu.VMEM)
    smem = pl.BlockSpec(memory_space=pltpu.SMEM)
    coef = pltpu.VMEM((cols + 4, levels, lat), f32)
    wind = pltpu.VMEM((cols + 2 * STEPS, levels, lat), f32)
    fields, update, misfit = pl.pallas_call(
        functools.partial(kernel, n_tile, n_trc),
        out_shape=(
            jax.ShapeDtypeStruct((levels, cols, group, lat), f32),
            jax.ShapeDtypeStruct((1, state), f32),
            jax.ShapeDtypeStruct((rows, LANES), f32),
        ),
        in_specs=[any_spec] * 3 + [smem, vmem, vmem, smem, vmem, vmem, vmem],
        out_specs=(any_spec, vmem, vmem),
        scratch_shapes=[
            pltpu.VMEM((levels, cols + 6, group, lat), f32),
            pltpu.VMEM((levels, cols + 4, group, lat), f32),
            pltpu.VMEM((levels, cols + 2, group, lat), f32),
            pltpu.VMEM((levels, cols, group, lat), f32),
            wind, wind, coef, coef, coef, coef,
            pltpu.VMEM((chunks, cols, lat, CHUNK), jnp.bfloat16),
            pltpu.VMEM((2, GROUP, group, cols * lat), jnp.bfloat16),
            pltpu.VMEM((n_trc, chunks, group, CHUNK), f32),
            pltpu.VMEM((ga, state, LANES), f32),
            pltpu.VMEM((gb, state, LANES), f32),
            dma((3,)), dma((levels,)),
            dma((levels,)), dma((levels,)), dma((levels,)), dma((levels,)),
            dma((4,)), dma((4,)),
            dma((max(1, n_trc - 1),)), dma((max(1, n_trc - 1),)),
            dma((max(1, ga - 1),)), dma((max(1, ga - 1),)),
            dma((max(1, gb - 1),)), dma((max(1, gb - 1),)),
        ],
        compiler_params=pltpu.CompilerParams(
            collective_id=0, has_side_effects=True, vmem_limit_bytes=56 * 1024 * 1024
        ),
    )(
        jnp.transpose(tracers, (1, 2, 0, 3)),
        jnp.transpose(courant, (1, 0, 2)),
        jnp.transpose(vertical_mix, (1, 0, 2)),
        kernel_profile,
        obs_cell.reshape(rows, LANES),
        obs_top.reshape(rows, LANES),
        obs_count,
        innovation.reshape(rows, LANES),
        obs_error.reshape(rows, LANES),
        prior_precision.reshape(1, state),
    )
    return (jnp.transpose(fields, (2, 0, 1, 3)), update.reshape(state), misfit.reshape(cap))


def solution(mesh):
    in_specs = (
        P("trc", None, "tile", None),
        P(None, "tile", None),
        P(None, "tile", None),
        P(),
        P("tile"),
        P("tile"),
        P("tile"),
        P("tile"),
        P("tile"),
        P(),
    )
    out_specs = (P("trc", None, "tile", None), P(), P("tile"))
    return jax.shard_map(
        functools.partial(per_device, mesh.shape["tile"], mesh.shape["trc"]),
        mesh=mesh, in_specs=in_specs, out_specs=out_specs, check_vma=False,
    )
```
